768 devices in a mesh: leaf: 192 (over z, y, core), sub: 4 (over x).
Axes of the slice: x: 4, y: 8, z: 12, core: 2. Of those that a mesh axis runs over, the one named last changes fastest.
Arguments:
- vectors: float32 [32, 786432], P(None, ('leaf', 'sub')), may hold values from -6 to 6
- bases: float32 [3072, 64, 256], P(('leaf', 'sub')), may hold values from -0.5 to 0.5
- transfers_leaf: float32 [768, 64, 256], P(('leaf', 'sub')), may hold values from -0.5 to 0.5
- transfers_group: float32 [768, 64, 64], P(('leaf', 'sub')), may hold values from -0.75 to 0.75
- near_blocks: float32 [3072, 256, 768], P(('leaf', 'sub')), may hold values from -0.21875 to 0.21875
- near_list: int32 [3072, 3], P(('leaf', 'sub')), may hold values from 0 to 47
- leaf_coupling: float32 [3072, 64, 384], P(('leaf', 'sub')), may hold values from -0.3125 to 0.3125
- leaf_list: int32 [3072, 6], P(('leaf', 'sub')), may hold values from 0 to 47
- leaf_count: int32 [3072], P(('leaf', 'sub')), may hold values from 1 to 6
- coarse_coupling: float32 [192, 64, 1024], P('leaf'), may hold values from -0.1875 to 0.1875
- coarse_list: int32 [192, 16], P('leaf'), may hold values from 0 to 191
- coarse_count: int32 [192], P('leaf'), may hold values from 1 to 16
Outputs:
- product: float32 [32, 786432], P(None, ('leaf', 'sub'))
The draws below stay inside these ranges and needn't reach their ends.
Inputs may be any that keep to these rules, and one draw needn't show every extreme that they name: `near_list`: the index of a source leaf among the 48 leaves of the group before the target leaf's group, its own group and the group after, in that order. `leaf_list`: the index of a source leaf among the 48 leaves of the group before the target leaf's group, its own group and the group after, in that order; entries at or beyond leaf_count are padding. `coarse_list`: entries at or beyond coarse_count are padding.
All inputs are finite; a program needn't handle non-finite values.
Results may differ from the reference program's by a relative error of at most 0.000068.
Values sent between devices are 32-bit elements; how exact they have to be, the bound alone decides.
A program may use at most 64 MiB of HBM per device.

```python
import jax
import jax.numpy as jnp
from jax import lax

RHS = 32
LEAF_SIZE = 256
RANK = 64
LEAF_DEV = 4
NEAR = 3
KA = 6
K2 = 16
GROUPS = 192
SUBS = 4
GROUP_LEAVES = 16
LEAVES = 3072
POINTS = 786432
N_LEAF = 192
N_SUB = 4


def place_ends(values, own_key, low, high):
    shape = values.shape
    index_at = [jax.random.randint(jax.random.fold_in(own_key, axis), (), 0, shape[axis]) for axis in range(len(shape))]
    values = values.at[tuple(index_at)].set(low)
    longest = shape.index(max(shape))
    index_at[longest] = (index_at[longest] + 1) % shape[longest]
    return values.at[tuple(index_at)].set(high)


def steps_of(rng, dims, split, smallest, high):
    loudness, own = 1.0, jax.random.fold_in(rng, 6)
    for dim, parts in split:
        heights = jnp.exp(jax.random.uniform(jax.random.fold_in(own, dim), (parts,), jnp.float32, smallest / len(split), high / len(split)))
        loudness = loudness * jnp.repeat(heights, dims[dim] // parts).reshape([-1 if axis == dim else 1 for axis in range(len(dims))])
    return loudness


def gaussian(rng, shape, scale, reach, split=(), kind=jnp.bfloat16):
    loudness = steps_of(rng, shape, split, -0.22, 0.18) if split else 1.0
    values = jax.random.normal(rng, shape, jnp.float32) * scale * loudness
    return jnp.minimum(jnp.maximum(values, -reach), reach).astype(kind)


def setup_inputs(seed: int = 0) -> dict:
    key_list = jax.random.split(jax.random.key(seed), 13)
    return {
        "vectors": gaussian(key_list[0], (RHS, POINTS), 1.0, 6.0, ((1, 768),), jnp.float32),
        "bases": gaussian(key_list[1], (LEAVES, RANK, LEAF_SIZE), (LEAF_SIZE // 2) ** -0.5, 0.5, ((0, 768),), jnp.float32),
        "transfers_leaf": gaussian(key_list[2], (N_LEAF * N_SUB, RANK, LEAF_DEV * RANK), (max(LEAF_DEV * RANK // 2, RANK // 2)) ** -0.5, 0.5, ((0, 768),), jnp.float32),
        "transfers_group": gaussian(key_list[3], (N_LEAF * N_SUB, RANK, RANK), RANK ** -0.5, 0.75, ((0, 768),), jnp.float32),
        "near_blocks": gaussian(key_list[4], (LEAVES, LEAF_SIZE, NEAR * LEAF_SIZE), (NEAR * LEAF_SIZE) ** -0.5, 0.21875, ((0, 768),), jnp.float32),
        "near_list": place_ends(jax.random.randint(key_list[5], (LEAVES, NEAR), 0, 3 * LEAF_DEV * N_SUB), jax.random.fold_in(key_list[5], 1), 0, (3 * LEAF_DEV * N_SUB) - 1).astype(jnp.int32),
        "leaf_coupling": gaussian(key_list[6], (LEAVES, RANK, KA * RANK), (KA * RANK) ** -0.5, 0.3125, ((0, 768),), jnp.float32),
        "leaf_list": place_ends(jax.random.randint(key_list[7], (LEAVES, KA), 0, 3 * LEAF_DEV * N_SUB), jax.random.fold_in(key_list[7], 1), 0, (3 * LEAF_DEV * N_SUB) - 1).astype(jnp.int32),
        "leaf_count": place_ends(jax.random.randint(key_list[8], (LEAVES,), 1, KA + 1), jax.random.fold_in(key_list[8], 1), 1, KA).astype(jnp.int32),
        "coarse_coupling": gaussian(key_list[9], (GROUPS, RANK, K2 * RANK), (K2 * RANK) ** -0.5, 0.1875, ((0, 192),), jnp.float32),
        "coarse_list": place_ends(jax.random.randint(key_list[10], (GROUPS, K2), 0, N_LEAF), jax.random.fold_in(key_list[10], 1), 0, N_LEAF - 1).astype(jnp.int32),
        "coarse_count": place_ends(jax.random.randint(key_list[11], (GROUPS,), 1, K2 + 1), jax.random.fold_in(key_list[11], 1), 1, K2).astype(jnp.int32),
    }


def reference(vectors, bases, transfers_leaf, transfers_group, near_blocks, near_list, leaf_coupling, leaf_list, leaf_count, coarse_coupling, coarse_list, coarse_count):
    highest = lax.Precision.HIGHEST
    device_total = N_LEAF * N_SUB
    blocks = vectors.reshape(RHS, LEAVES, LEAF_SIZE)
    leaf_coef = jnp.einsum('rlp,lap->rla', blocks, bases, precision=highest)
    grouped = leaf_coef.reshape(RHS, device_total, LEAF_DEV * RANK)
    device_coef = jnp.einsum('rdm,dam->rda', grouped, transfers_leaf, precision=highest)
    partial_coef = jnp.einsum('rdc,dac->rda', device_coef, transfers_group, precision=highest)
    group_coef = jnp.sum(partial_coef.reshape(RHS, GROUPS, SUBS, RANK), axis=2)
    coarse_mask = (jnp.arange(K2, dtype=jnp.int32)[None, :] < coarse_count[:, None]).astype(jnp.float32)
    coarse_picked = group_coef[:, coarse_list] * coarse_mask[None, :, :, None]
    coarse_field = jnp.einsum('rgkc,gakc->rga', coarse_picked, coarse_coupling.reshape(GROUPS, RANK, K2, RANK), precision=highest)
    owner_group = jnp.arange(device_total, dtype=jnp.int32) // SUBS
    device_field = jnp.einsum('rda,dac->rdc', coarse_field[:, owner_group], transfers_group, precision=highest)
    spread = jnp.einsum('rda,dam->rdm', device_field, transfers_leaf, precision=highest).reshape(RHS, LEAVES, RANK)
    base_leaf = (jnp.arange(LEAVES, dtype=jnp.int32) // GROUP_LEAVES - 1) * GROUP_LEAVES
    leaf_sources = (base_leaf[:, None] + leaf_list + LEAVES) % LEAVES
    leaf_mask = (jnp.arange(KA, dtype=jnp.int32)[None, :] < leaf_count[:, None]).astype(jnp.float32)
    leaf_picked = leaf_coef[:, leaf_sources] * leaf_mask[None, :, :, None]
    coupled = jnp.einsum('rlkc,lakc->rla', leaf_picked, leaf_coupling.reshape(LEAVES, RANK, KA, RANK), precision=highest)
    leaf_field = coupled + spread
    far_part = jnp.einsum('rla,lap->rlp', leaf_field, bases, precision=highest)
    near_sources = (base_leaf[:, None] + near_list + LEAVES) % LEAVES
    near_part = jnp.einsum('rlkp,lqkp->rlq', blocks[:, near_sources], near_blocks.reshape(LEAVES, LEAF_SIZE, NEAR, LEAF_SIZE), precision=highest)
    return (far_part + near_part).reshape(RHS, POINTS)
```

```python
import functools

import jax
import jax.numpy as jnp
from jax import lax
from jax.experimental import pallas as pl
from jax.experimental.pallas import tpu as pltpu
from jax.sharding import PartitionSpec as P

F32 = jnp.float32
BF16 = jnp.bfloat16
MESH = pl.DeviceIdType.MESH
ROWS = 32
PTS = 256
RANK = 64
SUBS = 4
CORES = 2
NY = 8
NZ = 12
KA = 6
NEAR = 3
K2 = 16
X_ORDER = (1, 3, 2)


def split(a):
    high = a.astype(BF16)
    return high, (a - high.astype(F32)).astype(BF16)


def dot(a, b, dim):
    return lax.dot_general(a, b, (((1,), (dim,)), ((), ())), preferred_element_type=F32)


def mul(a, b, dim):
    a_high, a_low = split(a)
    b_high, b_low = split(b)
    return dot(a_high, b_high, dim) + (dot(a_high, b_low, dim) + dot(a_low, b_high, dim))


def kernel(
    near_list,
    leaf_list,
    leaf_count,
    coarse_list,
    coarse_count,
    x_hbm,
    bases_hbm,
    tl_hbm,
    tg_hbm,
    near_hbm,
    la_hbm,
    ca_hbm,
    out_ref,
    xtab,
    ctab,
    bases,
    tl,
    tg,
    near,
    la,
    ca,
    mfold,
    pre,
    stage,
    rs_in,
    col,
    table,
    cf_stage,
    cf_all,
    load_sem,
    x_send,
    x_recv,
    rs_send,
    rs_recv,
    y_send,
    y_recv,
    z_send,
    z_recv,
    cf_send,
    cf_recv,
):
    leaf = lax.axis_index("leaf")
    s = lax.axis_index("sub")
    c = lax.rem(leaf, 2)
    y = lax.rem(lax.div(leaf, 2), NY)
    z = lax.div(leaf, 2 * NY)

    def leaf_of(zz, yy, cc):
        return zz * (2 * NY) + yy * 2 + cc

    def sub_at(d):
        return lax.rem(s + d, SUBS)

    sibling = leaf_of(z, y, 1 - c)
    partner = lax.rem(leaf + 192 + 2 * c - 1, 192)
    y_devs = [(leaf_of(z, lax.rem(y + d, NY), c), s) for d in range(1, NY)]

    loads = []

    def load(src, dst):
        cp = pltpu.make_async_copy(src, dst, load_sem.at[len(loads)])
        cp.start()
        loads.append(cp)
        return cp

    own = (SUBS + s) * 4
    x_loads = [
        load(x_hbm.at[:, pl.ds(j * PTS, PTS)], xtab.at[own + j]) for j in range(4)
    ]
    b_load = load(bases_hbm, bases)
    tl_load = load(tl_hbm, tl)
    tg_load = load(tg_hbm, tg)
    ca_load = load(ca_hbm, ca)
    la_load = load(la_hbm, la)
    near_load = load(near_hbm, near)

    barrier = pltpu.get_barrier_semaphore()
    met = 0

    def greet(dev):
        pl.semaphore_signal(barrier, inc=1, device_id=dev, device_id_type=MESH)

    for d in range(SUBS):
        for cc in range(2):
            if d == 0 and cc == 0:
                continue
            greet((leaf if cc == 0 else sibling, sub_at(d)))
            met += 1
    greet((partner, s))
    met += 1
    for dev in y_devs:
        greet(dev)
        met += 1
    for d in range(1, NZ):
        for cc in range(2):
            greet((leaf_of(lax.rem(z + d, NZ), y, c if cc == 0 else 1 - c), s))
            met += 1

    for cp in x_loads:
        cp.wait()
    b_load.wait()
    pairs = []
    for h in range(2):
        a0 = mul(xtab[own + 2 * h], bases[2 * h], 1)
        a1 = mul(xtab[own + 2 * h + 1], bases[2 * h + 1], 1)
        pairs.append(jnp.concatenate([a0, a1], axis=1))
    c_own = (SUBS + s) * 2
    for h in range(2):
        ctab[c_own + h] = pairs[h]
    tl_load.wait()
    tg_load.wait()
    fold = mul(tg[0], tl[0], 0)
    partial = mul(jnp.concatenate(pairs, axis=1), fold, 1)
    zero = jnp.zeros_like(partial)
    here = jnp.where(
        c == 0,
        jnp.concatenate([partial, zero], axis=1),
        jnp.concatenate([zero, partial], axis=1),
    )
    stage[...] = here.reshape(SUBS, 8, 128)

    pl.semaphore_wait(barrier, met)

    def remote(src, dst, send, recv, dev):
        return pltpu.make_async_remote_copy(
            src_ref=src,
            dst_ref=dst,
            send_sem=send,
            recv_sem=recv,
            device_id=dev,
            device_id_type=MESH,
        )

    sent = []

    def push(*args):
        cp = remote(*args)
        cp.start()
        sent.append(cp)
        return cp

    rs = []
    for d in range(SUBS):
        for cc in range(2):
            if d == 0 and cc == 0:
                continue
            to = sub_at(d)
            rs.append(
                push(
                    stage.at[to],
                    rs_in.at[d, cc],
                    rs_send.at[d, cc],
                    rs_recv.at[d, cc],
                    (leaf if cc == 0 else sibling, to),
                )
            )

    to_sibling = 2 * c
    to_partner = 2 - 2 * c

    def x_part(group, sub):
        return xtab.at[pl.ds((group * SUBS + sub) * 4, 4)]

    def c_part(group, sub):
        return ctab.at[pl.ds((group * SUBS + sub) * 2, 2)]

    def spread_block(d, sub):
        for i, part in enumerate((x_part, c_part)):
            push(part(1, sub), part(to_partner, sub), x_send.at[i, 2, d], x_recv.at[i, 2, d], (partner, s))
            push(part(1, sub), part(to_sibling, sub), x_send.at[i, 1, d], x_recv.at[i, 1, d], (sibling, s))

    for i, part in enumerate((x_part, c_part)):
        for d in X_ORDER:
            push(part(1, s), part(1, s), x_send.at[i, 0, d], x_recv.at[i, 0, d], (leaf, sub_at(d)))
    spread_block(0, s)

    for cp in rs:
        cp.wait_recv()
    tile = stage[s]
    for d in range(SUBS):
        for cc in range(2):
            if d == 0 and cc == 0:
                continue
            tile = tile + rs_in[d, cc]
    col[y] = tile
    ys = [
        push(col.at[y], col.at[y], y_send.at[i], y_recv.at[i], dev)
        for i, dev in enumerate(y_devs)
    ]

    for j in range(4):
        mfold[:, j * PTS : (j + 1) * PTS] = mul(fold[:, j * RANK : (j + 1) * RANK], bases[j], 0)

    for i in range(NY - 1):
        slot = col.at[lax.rem(y + NY - 1 - i, NY)]
        remote(slot, slot, y_send.at[i], y_recv.at[i], y_devs[i]).wait_recv()
    half = pl.ds(c * 4, 4)
    for d in range(1, NZ):
        for cc in range(2):
            push(
                col.at[half],
                table.at[z, half],
                z_send.at[d, cc],
                z_recv.at[d, cc],
                (leaf_of(lax.rem(z + d, NZ), y, c if cc == 0 else 1 - c), s),
            )
    table[z] = col[...]

    def arrived(i, way, d, ref):
        remote(ref, ref, x_send.at[i, way, d], x_recv.at[i, way, d], (sibling, s)).wait_recv()

    for d in X_ORDER:
        sub = lax.rem(s + SUBS - d, SUBS)
        arrived(0, 0, d, x_part(1, sub))
        arrived(1, 0, d, c_part(1, sub))
        spread_block(d, sub)
    for d in range(SUBS):
        sub = lax.rem(s + SUBS - d, SUBS)
        for i, part in enumerate((x_part, c_part)):
            arrived(i, 1, d, part(2 - 2 * c, sub))
            arrived(i, 2, d, part(2 * c, sub))

    lane = lax.broadcasted_iota(jnp.int32, (ROWS, 128), 1)

    def picked(tab, entry, k, use):
        both = tab[lax.div(entry, 2)]
        turned = pltpu.roll(both, 64, 1)
        keep = jnp.where(lax.rem(entry, 2) == k % 2, 1.0, 0.0) * use
        turn = use - keep
        return both * keep + turned * turn

    la_load.wait()
    near_load.wait()
    for j in range(4):
        pieces = []
        for k in range(0, KA, 2):
            lo, hi = (
                picked(ctab, leaf_list[j, q], q, jnp.where(q < leaf_count[j], 1.0, 0.0))
                for q in (k, k + 1)
            )
            pieces.append(jnp.where(lane < RANK, lo, hi))
        coupled = mul(jnp.concatenate(pieces, axis=1), la[j], 1)
        far = mul(coupled, bases[j], 0)
        sources = jnp.concatenate([xtab[near_list[j, k]] for k in range(NEAR)], axis=1)
        pre[:, j * PTS : (j + 1) * PTS] = far + mul(sources, near[j], 1)

    for d in range(1, NZ):
        zz = lax.rem(z + NZ - d, NZ)
        for cc in range(2):
            part = table.at[zz, pl.ds((c if cc == 0 else 1 - c) * 4, 4)]
            remote(part, part, z_send.at[d, cc], z_recv.at[d, cc], (sibling, s)).wait_recv()
    ca_load.wait()
    lane8 = lax.broadcasted_iota(jnp.int32, (8, 128), 1)
    pieces = []
    for k in range(0, K2, 2):
        two = []
        for q in (k, k + 1):
            entry = coarse_list[0, q]
            chip = lax.div(entry, 2)
            both = table[lax.div(chip, NY), lax.rem(chip, NY)]
            turned = pltpu.roll(both, 64, 1)
            use = jnp.where(q < coarse_count[0], 1.0, 0.0)
            keep = jnp.where(lax.rem(entry, 2) == q % 2, 1.0, 0.0) * use
            two.append(both * keep + turned * (use - keep))
        pieces.append(jnp.where(lane8 < RANK, two[0], two[1]))
    field = mul(jnp.concatenate(pieces, axis=1), ca[0], 1)
    cf_all[s] = jnp.concatenate([field, jnp.zeros_like(field)], axis=1)
    cfs = [
        push(cf_all.at[s], cf_all.at[s], cf_send.at[d], cf_recv.at[d], (leaf, sub_at(d)))
        for d in range(1, SUBS)
    ]
    for d in range(1, SUBS):
        slot = cf_all.at[lax.rem(s + SUBS - d, SUBS)]
        remote(slot, slot, cf_send.at[d], cf_recv.at[d], (sibling, s)).wait_recv()
    field_all = cf_all[...].reshape(ROWS, 128)[:, :RANK]
    out_ref[...] = pre[...] + mul(field_all, mfold[...], 0)

    for cp in sent:
        cp.wait_send()


def per_device(
    vectors,
    bases,
    transfers_leaf,
    transfers_group,
    near_blocks,
    near_list,
    leaf_coupling,
    leaf_list,
    leaf_count,
    coarse_coupling,
    coarse_list,
    coarse_count,
):
    smem = pl.BlockSpec(memory_space=pltpu.SMEM)
    anywhere = pl.BlockSpec(memory_space=pl.ANY)
    dma = pltpu.SemaphoreType.DMA
    return pl.pallas_call(
        kernel,
        out_shape=jax.ShapeDtypeStruct(vectors.shape, F32),
        in_specs=[smem] * 5 + [anywhere] * 7,
        out_specs=pl.BlockSpec(memory_space=pltpu.VMEM),
        scratch_shapes=[
            pltpu.VMEM((48, ROWS, PTS), F32),
            pltpu.VMEM((24, ROWS, 128), F32),
            pltpu.VMEM(bases.shape, F32),
            pltpu.VMEM(transfers_leaf.shape, F32),
            pltpu.VMEM(transfers_group.shape, F32),
            pltpu.VMEM(near_blocks.shape, F32),
            pltpu.VMEM(leaf_coupling.shape, F32),
            pltpu.VMEM(coarse_coupling.shape, F32),
            pltpu.VMEM((RANK, 4 * PTS), F32),
            pltpu.VMEM((ROWS, 4 * PTS), F32),
            pltpu.VMEM((SUBS, 8, 128), F32),
            pltpu.VMEM((SUBS, 2, 8, 128), F32),
            pltpu.VMEM((NY, 8, 128), F32),
            pltpu.VMEM((NZ, NY, 8, 128), F32),
            pltpu.VMEM((8, 128), F32),
            pltpu.VMEM((SUBS, 8, 128), F32),
            dma((10,)),
            dma((2, 3, SUBS)),
            dma((2, 3, SUBS)),
            dma((SUBS, 2)),
            dma((SUBS, 2)),
            dma((NY - 1,)),
            dma((NY - 1,)),
            dma((NZ, 2)),
            dma((NZ, 2)),
            dma((SUBS,)),
            dma((SUBS,)),
        ],
        compiler_params=pltpu.CompilerParams(
            collective_id=0, has_side_effects=True, vmem_limit_bytes=40 * 1024 * 1024
        ),
    )(
        near_list,
        leaf_list,
        leaf_count,
        coarse_list,
        coarse_count,
        vectors,
        bases,
        transfers_leaf,
        transfers_group,
        near_blocks,
        leaf_coupling,
        coarse_coupling,
    )


def solution(mesh):
    return jax.shard_map(
        per_device,
        mesh=mesh,
        in_specs=(
            P(None, ("leaf", "sub")),
            P(("leaf", "sub"), None, None),
            P(("leaf", "sub"), None, None),
            P(("leaf", "sub"), None, None),
            P(("leaf", "sub"), None, None),
            P(("leaf", "sub"), None),
            P(("leaf", "sub"), None, None),
            P(("leaf", "sub"), None),
            P(("leaf", "sub")),
            P("leaf", None, None),
            P("leaf", None),
            P("leaf"),
        ),
        out_specs=P(None, ("leaf", "sub")),
        check_vma=False,
    )
```

```python
import functools

import jax
import jax.numpy as jnp
from jax import lax
from jax.experimental import pallas as pl
from jax.experimental.pallas import tpu as pltpu
from jax.sharding import PartitionSpec as P

F32 = jnp.float32
BF16 = jnp.bfloat16
MESH = pl.DeviceIdType.MESH
ROWS = 32
PTS = 256
RANK = 64
SUBS = 4
CORES = 2
NY = 8
NZ = 12
KA = 6
NEAR = 3
K2 = 16
X_ORDER = (1, 3, 2)


def split(a):
    high = a.astype(BF16)
    return high, (a - high.astype(F32)).astype(BF16)


def dot(a, b, dim):
    return lax.dot_general(a, b, (((1,), (dim,)), ((), ())), preferred_element_type=F32)


def mul(a, b, dim):
    a_high, a_low = split(a)
    b_high, b_low = split(b)
    return dot(a_high, b_high, dim) + (dot(a_high, b_low, dim) + dot(a_low, b_high, dim))


def kernel(
    near_list_hbm,
    leaf_list_hbm,
    leaf_count_hbm,
    coarse_list_hbm,
    coarse_count_hbm,
    x_hbm,
    bases_hbm,
    tl_hbm,
    tg_hbm,
    near_hbm,
    la_hbm,
    ca_hbm,
    out_ref,
    near_list,
    leaf_list,
    leaf_count,
    coarse_list,
    coarse_count,
    xtab,
    ctab,
    bases,
    tl,
    tg,
    near,
    la,
    ca,
    mfold,
    pre,
    stage,
    rs_in,
    mine,
    table,
    cf_all,
    load_sem,
    x_send,
    x_recv,
    rs_send,
    rs_recv,
    z_send,
    z_recv,
    s_send,
    s_recv,
    cf_send,
    cf_recv,
):
    leaf = lax.axis_index("leaf")
    s = lax.axis_index("sub")
    c = lax.rem(leaf, 2)
    y = lax.rem(lax.div(leaf, 2), NY)
    z = lax.div(leaf, 2 * NY)

    def leaf_of(zz, yy, cc):
        return zz * (2 * NY) + yy * 2 + cc

    def sub_at(d):
        return lax.rem(s + d, SUBS)

    sibling = leaf_of(z, y, 1 - c)
    partner = lax.rem(leaf + 192 + 2 * c - 1, 192)
    row = [(d, cc) for d in range(SUBS) for cc in range(CORES) if d + cc]

    def row_dev(d, cc):
        return (sibling if cc else leaf, sub_at(d))

    def plane_dev(i, dy):
        return (leaf_of(lax.rem(z + 2 * i + c, NZ), lax.rem(y + dy, NY), c), s)

    def far_first(pair):
        i, dy = pair
        z_hops = min(2 * i, NZ - 2 * i) + min(2 * i + 1, NZ - 2 * i - 1)
        return -(z_hops / 2 + min(dy, NY - dy))

    plane = sorted(
        ((i, dy) for i in range(NZ // 2) for dy in range(NY) if i + dy), key=far_first
    )

    loads = {}

    def load(name, src, dst):
        loads[name] = pltpu.make_async_copy(src, dst, load_sem.at[len(loads)])
        loads[name].start()

    own = (SUBS + s) * 4
    for j in range(4):
        load("x%d" % j, x_hbm.at[:, pl.ds(j * PTS, PTS)], xtab.at[own + j])
    load("bases", bases_hbm, bases)
    load("tl", tl_hbm, tl)
    load("tg", tg_hbm, tg)

    barrier = pltpu.get_barrier_semaphore()

    def greet(dev):
        pl.semaphore_signal(barrier, inc=1, device_id=dev, device_id_type=MESH)

    def back(i, dy):
        return (leaf_of(lax.rem(z + NZ - 2 * i - c, NZ), lax.rem(y + NY - dy, NY), c), s)

    for d, cc in row:
        greet(row_dev(d, cc))
    greet((partner, s))
    for i, dy in plane:
        greet(back(i, dy))

    @pl.when(c == 1)
    def _():
        greet(back(0, 0))

    for j in range(4):
        loads["x%d" % j].wait()
    loads["bases"].wait()
    pairs = []
    for h in range(2):
        a0 = mul(xtab[own + 2 * h], bases[2 * h], 1)
        a1 = mul(xtab[own + 2 * h + 1], bases[2 * h + 1], 1)
        pairs.append(jnp.concatenate([a0, a1], axis=1))
    c_own = (SUBS + s) * 2
    for h in range(2):
        ctab[c_own + h] = pairs[h]
    loads["tl"].wait()
    loads["tg"].wait()
    fold = mul(tg[0], tl[0], 0)
    partial = mul(jnp.concatenate(pairs, axis=1), fold, 1)
    zero = jnp.zeros_like(partial)
    here = jnp.where(
        c == 0,
        jnp.concatenate([partial, zero], axis=1),
        jnp.concatenate([zero, partial], axis=1),
    )
    stage[...] = here.reshape(SUBS, 8, 128)

    pl.semaphore_wait(barrier, len(row) + 1 + len(plane) + c)

    def remote(src, dst, send, recv, dev):
        return pltpu.make_async_remote_copy(
            src_ref=src,
            dst_ref=dst,
            send_sem=send,
            recv_sem=recv,
            device_id=dev,
            device_id_type=MESH,
        )

    sent = []

    def push(*args):
        cp = remote(*args)
        cp.start()
        sent.append(cp)
        return cp

    rs = [
        push(
            stage.at[sub_at(d)],
            rs_in.at[d, cc],
            rs_send.at[d, cc],
            rs_recv.at[d, cc],
            row_dev(d, cc),
        )
        for d, cc in row
    ]

    to_sibling = 2 * c
    to_partner = 2 - 2 * c

    def x_part(group, sub):
        return xtab.at[pl.ds((group * SUBS + sub) * 4, 4)]

    def c_part(group, sub):
        return ctab.at[pl.ds((group * SUBS + sub) * 2, 2)]

    def spread_block(d, sub):
        for i, part in enumerate((x_part, c_part)):
            push(part(1, sub), part(to_partner, sub), x_send.at[i, 2, d], x_recv.at[i, 2, d], (partner, s))
            push(part(1, sub), part(to_sibling, sub), x_send.at[i, 1, d], x_recv.at[i, 1, d], (sibling, s))

    for i, part in enumerate((x_part, c_part)):
        for d in X_ORDER:
            push(part(1, s), part(1, s), x_send.at[i, 0, d], x_recv.at[i, 0, d], (leaf, sub_at(d)))
    spread_block(0, s)

    load("ca", ca_hbm, ca)
    load("la", la_hbm, la)
    load("near", near_hbm, near)
    lists = (
        (near_list_hbm, near_list),
        (leaf_list_hbm, leaf_list),
        (leaf_count_hbm, leaf_count),
        (coarse_list_hbm, coarse_list),
        (coarse_count_hbm, coarse_count),
    )
    for i, (src, dst) in enumerate(lists):
        load("list%d" % i, src, dst)

    for cp in rs:
        cp.wait_recv()
    tile = stage[s]
    for d, cc in row:
        tile = tile + rs_in[d, cc]
    mine[...] = tile

    @pl.when(c == 0)
    def _():
        table[z, y] = tile

    for i, dy in plane:
        remote(mine, table.at[z, y], z_send.at[i], z_recv.at[i], plane_dev(i, dy)).start()

    @pl.when(c == 1)
    def _():
        remote(mine, table.at[z, y], z_send.at[0], z_recv.at[0], plane_dev(0, 0)).start()

    for j in range(4):
        mfold[:, j * PTS : (j + 1) * PTS] = mul(fold[:, j * RANK : (j + 1) * RANK], bases[j], 0)

    def arrived(i, way, d, ref):
        remote(ref, ref, x_send.at[i, way, d], x_recv.at[i, way, d], (sibling, s)).wait_recv()

    for d in X_ORDER:
        sub = lax.rem(s + SUBS - d, SUBS)
        arrived(0, 0, d, x_part(1, sub))
        arrived(1, 0, d, c_part(1, sub))
        spread_block(d, sub)

    def tiles_in(i, count):
        ref = table.at[0, pl.ds(0, count)]
        return remote(ref, ref, z_send.at[i], z_recv.at[i], (sibling, s))

    def own_tiles(wait):
        @pl.when(c == 1)
        def _():
            wait(tiles_in(0, NY))

        @pl.when(c == 0)
        def _():
            wait(tiles_in(0, NY - 1))

    for i in (0, 5, 1, 4, 2, 3):
        if i:
            tiles_in(i, NY).wait_recv()
        else:
            own_tiles(lambda cp: cp.wait_recv())
        part = table.at[lax.rem(z + NZ - 2 * i - c, NZ)]
        push(part, part, s_send.at[i], s_recv.at[i], (sibling, s))

    for i in range(len(lists)):
        loads["list%d" % i].wait()
    loads["ca"].wait()
    for i in range(NZ // 2):
        part = table.at[lax.rem(z + NZ - 2 * i - 1 + c, NZ)]
        remote(part, part, s_send.at[i], s_recv.at[i], (sibling, s)).wait_recv()
    lane8 = lax.broadcasted_iota(jnp.int32, (8, 128), 1)
    pieces = []
    for k in range(0, K2, 2):
        two = []
        for q in (k, k + 1):
            entry = coarse_list[0, q]
            chip = lax.div(entry, 2)
            both = table[lax.div(chip, NY), lax.rem(chip, NY)]
            turned = pltpu.roll(both, 64, 1)
            use = jnp.where(q < coarse_count[0], 1.0, 0.0)
            keep = jnp.where(lax.rem(entry, 2) == q % 2, 1.0, 0.0) * use
            two.append(both * keep + turned * (use - keep))
        pieces.append(jnp.where(lane8 < RANK, two[0], two[1]))
    field = mul(jnp.concatenate(pieces, axis=1), ca[0], 1)
    cf_all[s] = jnp.concatenate([field, jnp.zeros_like(field)], axis=1)
    for d in range(1, SUBS):
        push(cf_all.at[s], cf_all.at[s], cf_send.at[d], cf_recv.at[d], (leaf, sub_at(d)))

    for d in range(SUBS):
        sub = lax.rem(s + SUBS - d, SUBS)
        for i, part in enumerate((x_part, c_part)):
            arrived(i, 1, d, part(2 - 2 * c, sub))
            arrived(i, 2, d, part(2 * c, sub))
    lane = lax.broadcasted_iota(jnp.int32, (ROWS, 128), 1)

    def picked(entry, k, use):
        both = ctab[lax.div(entry, 2)]
        turned = pltpu.roll(both, 64, 1)
        keep = jnp.where(lax.rem(entry, 2) == k % 2, 1.0, 0.0) * use
        return both * keep + turned * (use - keep)

    loads["la"].wait()
    loads["near"].wait()
    for j in range(4):
        pieces = []
        for k in range(0, KA, 2):
            lo, hi = (
                picked(leaf_list[j, q], q, jnp.where(q < leaf_count[j], 1.0, 0.0))
                for q in (k, k + 1)
            )
            pieces.append(jnp.where(lane < RANK, lo, hi))
        coupled = mul(jnp.concatenate(pieces, axis=1), la[j], 1)
        far = mul(coupled, bases[j], 0)
        sources = jnp.concatenate([xtab[near_list[j, k]] for k in range(NEAR)], axis=1)
        pre[:, j * PTS : (j + 1) * PTS] = far + mul(sources, near[j], 1)

    for d in range(1, SUBS):
        slot = cf_all.at[lax.rem(s + SUBS - d, SUBS)]
        remote(slot, slot, cf_send.at[d], cf_recv.at[d], (sibling, s)).wait_recv()
    field_all = cf_all[...].reshape(ROWS, 128)[:, :RANK]
    out_ref[...] = pre[...] + mul(field_all, mfold[...], 0)

    for cp in sent:
        cp.wait_send()
    for i in range(1, NZ // 2):
        tiles_in(i, NY).wait_send()
    own_tiles(lambda cp: cp.wait_send())


def per_device(
    vectors,
    bases,
    transfers_leaf,
    transfers_group,
    near_blocks,
    near_list,
    leaf_coupling,
    leaf_list,
    leaf_count,
    coarse_coupling,
    coarse_list,
    coarse_count,
):
    in_hbm = pl.BlockSpec(memory_space=pltpu.HBM)
    dma = pltpu.SemaphoreType.DMA
    return pl.pallas_call(
        kernel,
        out_shape=jax.ShapeDtypeStruct(vectors.shape, F32),
        in_specs=[in_hbm] * 12,
        out_specs=pl.BlockSpec(memory_space=pltpu.VMEM),
        scratch_shapes=[
            pltpu.SMEM(near_list.shape, jnp.int32),
            pltpu.SMEM(leaf_list.shape, jnp.int32),
            pltpu.SMEM(leaf_count.shape, jnp.int32),
            pltpu.SMEM(coarse_list.shape, jnp.int32),
            pltpu.SMEM(coarse_count.shape, jnp.int32),
            pltpu.VMEM((48, ROWS, PTS), F32),
            pltpu.VMEM((24, ROWS, 128), F32),
            pltpu.VMEM(bases.shape, F32),
            pltpu.VMEM(transfers_leaf.shape, F32),
            pltpu.VMEM(transfers_group.shape, F32),
            pltpu.VMEM(near_blocks.shape, F32),
            pltpu.VMEM(leaf_coupling.shape, F32),
            pltpu.VMEM(coarse_coupling.shape, F32),
            pltpu.VMEM((RANK, 4 * PTS), F32),
            pltpu.VMEM((ROWS, 4 * PTS), F32),
            pltpu.VMEM((SUBS, 8, 128), F32),
            pltpu.VMEM((SUBS, 2, 8, 128), F32),
            pltpu.VMEM((8, 128), F32),
            pltpu.VMEM((NZ, NY, 8, 128), F32),
            pltpu.VMEM((SUBS, 8, 128), F32),
            dma((15,)),
            dma((2, 3, SUBS)),
            dma((2, 3, SUBS)),
            dma((SUBS, 2)),
            dma((SUBS, 2)),
            dma((NZ // 2,)),
            dma((NZ // 2,)),
            dma((NZ // 2,)),
            dma((NZ // 2,)),
            dma((SUBS,)),
            dma((SUBS,)),
        ],
        compiler_params=pltpu.CompilerParams(
            collective_id=0, has_side_effects=True, vmem_limit_bytes=60 * 1024 * 1024
        ),
    )(
        near_list,
        leaf_list,
        leaf_count,
        coarse_list,
        coarse_count,
        vectors,
        bases,
        transfers_leaf,
        transfers_group,
        near_blocks,
        leaf_coupling,
        coarse_coupling,
    )


def solution(mesh):
    return jax.shard_map(
        per_device,
        mesh=mesh,
        in_specs=(
            P(None, ("leaf", "sub")),
            P(("leaf", "sub"), None, None),
            P(("leaf", "sub"), None, None),
            P(("leaf", "sub"), None, None),
            P(("leaf", "sub"), None, None),
            P(("leaf", "sub"), None),
            P(("leaf", "sub"), None, None),
            P(("leaf", "sub"), None),
            P(("leaf", "sub")),
            P("leaf", None, None),
            P("leaf", None),
            P("leaf"),
        ),
        out_specs=P(None, ("leaf", "sub")),
        check_vma=False,
    )
```

```python
import functools

import jax
import jax.numpy as jnp
from jax import lax
from jax.experimental import pallas as pl
from jax.experimental.pallas import tpu as pltpu
from jax.sharding import PartitionSpec as P

F32 = jnp.float32
BF16 = jnp.bfloat16
MESH = pl.DeviceIdType.MESH
ROWS = 32
PTS = 256
RANK = 64
SUBS = 4
CORES = 2
NY = 8
NZ = 12
KA = 6
NEAR = 3
K2 = 16
X_ORDER = (1, 3, 2)
DYS = (4, 3, 5, 2, 6, 1, 7)


def split(a):
    high = a.astype(BF16)
    return high, (a - high.astype(F32)).astype(BF16)


def dot(a, b, dim):
    return lax.dot_general(a, b, (((1,), (dim,)), ((), ())), preferred_element_type=F32)


def mul(a, b, dim):
    a_high, a_low = split(a)
    b_high, b_low = split(b)
    return dot(a_high, b_high, dim) + (dot(a_high, b_low, dim) + dot(a_low, b_high, dim))


def kernel(
    near_list_hbm,
    leaf_list_hbm,
    leaf_count_hbm,
    coarse_list_hbm,
    coarse_count_hbm,
    x_hbm,
    bases_hbm,
    tl_hbm,
    tg_hbm,
    near_hbm,
    la_hbm,
    ca_hbm,
    out_ref,
    near_list,
    leaf_list,
    leaf_count,
    coarse_list,
    coarse_count,
    xtab,
    ctab,
    bases,
    tl,
    tg,
    near,
    la,
    ca,
    mfold,
    pre,
    stage,
    rs_in,
    mine,
    table,
    cf_all,
    seen,
    load_sem,
    x_send,
    x_recv,
    rs_send,
    rs_recv,
    z_send,
    z_recv,
    s_send,
    s_recv,
    cf_send,
    cf_recv,
):
    leaf = lax.axis_index("leaf")
    s = lax.axis_index("sub")
    c = lax.rem(leaf, 2)
    y = lax.rem(lax.div(leaf, 2), NY)
    z = lax.div(leaf, 2 * NY)

    def leaf_of(zz, yy, cc):
        return zz * (2 * NY) + yy * 2 + cc

    def sub_at(d):
        return lax.rem(s + d, SUBS)

    sibling = leaf_of(z, y, 1 - c)
    partner = lax.rem(leaf + 192 + 2 * c - 1, 192)
    row = [(d, cc) for d in range(SUBS) for cc in range(CORES) if d + cc]

    def row_dev(d, cc):
        return (sibling if cc else leaf, sub_at(d))

    def plane_dev(p, dy):
        return (leaf_of(p, lax.rem(y + dy, NY), c), s)

    first = lax.rem(z + c, 2)
    below = lax.div(z + c, 2)

    loads = {}

    def load(name, src, dst):
        loads[name] = pltpu.make_async_copy(src, dst, load_sem.at[len(loads)])
        loads[name].start()

    own = (SUBS + s) * 4
    for j in range(4):
        load("x%d" % j, x_hbm.at[:, pl.ds(j * PTS, PTS)], xtab.at[own + j])
    load("bases", bases_hbm, bases)
    load("tl", tl_hbm, tl)
    load("tg", tg_hbm, tg)

    barrier = pltpu.get_barrier_semaphore()

    def greet(dev):
        pl.semaphore_signal(barrier, inc=1, device_id=dev, device_id_type=MESH)

    for d, cc in row:
        greet(row_dev(d, cc))
    greet((partner, s))

    @pl.when(c == 0)
    def _():
        for dy in range(1, NY):
            greet(plane_dev(z, dy))

    def greet_plane(q, carry):
        for dy in range(NY):
            greet(plane_dev(first + 2 * q, dy))
        return carry

    lax.fori_loop(below + 1 - c, NZ // 2, greet_plane, 0)

    for j in range(4):
        loads["x%d" % j].wait()
    loads["bases"].wait()
    pairs = []
    for h in range(2):
        a0 = mul(xtab[own + 2 * h], bases[2 * h], 1)
        a1 = mul(xtab[own + 2 * h + 1], bases[2 * h + 1], 1)
        pairs.append(jnp.concatenate([a0, a1], axis=1))
    c_own = (SUBS + s) * 2
    for h in range(2):
        ctab[c_own + h] = pairs[h]
    loads["tl"].wait()
    loads["tg"].wait()
    fold = mul(tg[0], tl[0], 0)
    partial = mul(jnp.concatenate(pairs, axis=1), fold, 1)
    zero = jnp.zeros_like(partial)
    here = jnp.where(
        c == 0,
        jnp.concatenate([partial, zero], axis=1),
        jnp.concatenate([zero, partial], axis=1),
    )
    stage[...] = here.reshape(SUBS, 8, 128)

    pl.semaphore_wait(barrier, len(row) + 1 + (1 - c) * (NY - 1) + below * NY)

    def remote(src, dst, send, recv, dev):
        return pltpu.make_async_remote_copy(
            src_ref=src,
            dst_ref=dst,
            send_sem=send,
            recv_sem=recv,
            device_id=dev,
            device_id_type=MESH,
        )

    sent = []

    def push(*args):
        cp = remote(*args)
        cp.start()
        sent.append(cp)
        return cp

    rs = [
        push(
            stage.at[sub_at(d)],
            rs_in.at[d, cc],
            rs_send.at[d, cc],
            rs_recv.at[d, cc],
            row_dev(d, cc),
        )
        for d, cc in row
    ]

    to_sibling = 2 * c
    to_partner = 2 - 2 * c

    def x_part(group, sub):
        return xtab.at[pl.ds((group * SUBS + sub) * 4, 4)]

    def c_part(group, sub):
        return ctab.at[pl.ds((group * SUBS + sub) * 2, 2)]

    def spread_block(d, sub):
        for i, part in enumerate((x_part, c_part)):
            push(part(1, sub), part(to_partner, sub), x_send.at[i, 2, d], x_recv.at[i, 2, d], (partner, s))
            push(part(1, sub), part(to_sibling, sub), x_send.at[i, 1, d], x_recv.at[i, 1, d], (sibling, s))

    for i, part in enumerate((x_part, c_part)):
        for d in X_ORDER:
            push(part(1, s), part(1, s), x_send.at[i, 0, d], x_recv.at[i, 0, d], (leaf, sub_at(d)))
    spread_block(0, s)

    def tell_plane(q, carry):
        for dy in range(NY):
            pl.semaphore_signal(
                seen.at[lax.div(z, 2)],
                inc=1,
                device_id=plane_dev(first + 2 * q, dy),
                device_id_type=MESH,
            )
        return carry

    lax.fori_loop(0, below, tell_plane, 0)

    load("ca", ca_hbm, ca)
    load("la", la_hbm, la)
    load("near", near_hbm, near)
    lists = (
        (near_list_hbm, near_list),
        (leaf_list_hbm, leaf_list),
        (leaf_count_hbm, leaf_count),
        (coarse_list_hbm, coarse_list),
        (coarse_count_hbm, coarse_count),
    )
    for i, (src, dst) in enumerate(lists):
        load("list%d" % i, src, dst)

    for cp in rs:
        cp.wait_recv()
    tile = stage[s]
    for d, cc in row:
        tile = tile + rs_in[d, cc]
    mine[...] = tile

    @pl.when(c == 0)
    def _():
        table[z, y] = tile

    def tile_to(p, dys):
        half = lax.div(p, 2)
        for dy in dys:
            remote(mine, table.at[z, y], z_send.at[half], z_recv.at[lax.div(z, 2)], plane_dev(p, dy)).start()

    def tile_below(q, carry):
        tile_to(first + 2 * q, DYS + (0,))
        return carry

    lax.fori_loop(0, below, tile_below, 0)

    @pl.when(c == 0)
    def _():
        tile_to(z, DYS)

    for j in range(4):
        mfold[:, j * PTS : (j + 1) * PTS] = mul(fold[:, j * RANK : (j + 1) * RANK], bases[j], 0)

    def arrived(i, way, d, ref):
        remote(ref, ref, x_send.at[i, way, d], x_recv.at[i, way, d], (sibling, s)).wait_recv()

    for d in X_ORDER:
        sub = lax.rem(s + SUBS - d, SUBS)
        arrived(0, 0, d, x_part(1, sub))
        arrived(1, 0, d, c_part(1, sub))
        spread_block(d, sub)

    def tiles_at(p, count):
        ref = table.at[0, pl.ds(0, count)]
        half = lax.div(p, 2)
        return remote(ref, ref, z_send.at[half], z_recv.at[half], (sibling, s))

    def own_plane(wait):
        @pl.when(c == 0)
        def _():
            wait(tiles_at(z, NY - 1))

    for i in range(NZ // 2):
        p = z + 2 * i + c

        @pl.when((p > z) & (p < NZ))
        def _():
            pl.semaphore_wait(seen.at[lax.div(p, 2)], NY)
            tile_to(p, DYS + (0,))

    for i in range(NZ // 2):
        p = lax.rem(z + 2 * i + c, NZ)
        if i:
            tiles_at(p, NY).wait_recv()
        else:
            own_plane(lambda cp: cp.wait_recv())

            @pl.when(c == 1)
            def _():
                tiles_at(p, NY).wait_recv()

        part = table.at[p]
        push(part, part, s_send.at[i], s_recv.at[i], (sibling, s))

    for i in range(len(lists)):
        loads["list%d" % i].wait()
    loads["ca"].wait()
    for i in range(NZ // 2):
        part = table.at[lax.rem(z + 2 * i + 1 - c, NZ)]
        remote(part, part, s_send.at[i], s_recv.at[i], (sibling, s)).wait_recv()
    lane8 = lax.broadcasted_iota(jnp.int32, (8, 128), 1)
    pieces = []
    for k in range(0, K2, 2):
        two = []
        for q in (k, k + 1):
            entry = coarse_list[0, q]
            chip = lax.div(entry, 2)
            both = table[lax.div(chip, NY), lax.rem(chip, NY)]
            turned = pltpu.roll(both, 64, 1)
            use = jnp.where(q < coarse_count[0], 1.0, 0.0)
            keep = jnp.where(lax.rem(entry, 2) == q % 2, 1.0, 0.0) * use
            two.append(both * keep + turned * (use - keep))
        pieces.append(jnp.where(lane8 < RANK, two[0], two[1]))
    field = mul(jnp.concatenate(pieces, axis=1), ca[0], 1)
    cf_all[s] = jnp.concatenate([field, jnp.zeros_like(field)], axis=1)
    for d in range(1, SUBS):
        push(cf_all.at[s], cf_all.at[s], cf_send.at[d], cf_recv.at[d], (leaf, sub_at(d)))

    for d in range(SUBS):
        sub = lax.rem(s + SUBS - d, SUBS)
        for i, part in enumerate((x_part, c_part)):
            arrived(i, 1, d, part(2 - 2 * c, sub))
            arrived(i, 2, d, part(2 * c, sub))
    lane = lax.broadcasted_iota(jnp.int32, (ROWS, 128), 1)

    def picked(entry, k, use):
        both = ctab[lax.div(entry, 2)]
        turned = pltpu.roll(both, 64, 1)
        keep = jnp.where(lax.rem(entry, 2) == k % 2, 1.0, 0.0) * use
        return both * keep + turned * (use - keep)

    loads["la"].wait()
    loads["near"].wait()
    for j in range(4):
        pieces = []
        for k in range(0, KA, 2):
            lo, hi = (
                picked(leaf_list[j, q], q, jnp.where(q < leaf_count[j], 1.0, 0.0))
                for q in (k, k + 1)
            )
            pieces.append(jnp.where(lane < RANK, lo, hi))
        coupled = mul(jnp.concatenate(pieces, axis=1), la[j], 1)
        far = mul(coupled, bases[j], 0)
        sources = jnp.concatenate([xtab[near_list[j, k]] for k in range(NEAR)], axis=1)
        pre[:, j * PTS : (j + 1) * PTS] = far + mul(sources, near[j], 1)

    for d in range(1, SUBS):
        slot = cf_all.at[lax.rem(s + SUBS - d, SUBS)]
        remote(slot, slot, cf_send.at[d], cf_recv.at[d], (sibling, s)).wait_recv()
    field_all = cf_all[...].reshape(ROWS, 128)[:, :RANK]
    out_ref[...] = pre[...] + mul(field_all, mfold[...], 0)

    for cp in sent:
        cp.wait_send()
    for i in range(NZ // 2):
        if i:
            tiles_at(lax.rem(z + 2 * i + c, NZ), NY).wait_send()
        else:
            own_plane(lambda cp: cp.wait_send())

            @pl.when(c == 1)
            def _():
                tiles_at(lax.rem(z + 1, NZ), NY).wait_send()


def per_device(
    vectors,
    bases,
    transfers_leaf,
    transfers_group,
    near_blocks,
    near_list,
    leaf_coupling,
    leaf_list,
    leaf_count,
    coarse_coupling,
    coarse_list,
    coarse_count,
):
    in_hbm = pl.BlockSpec(memory_space=pltpu.HBM)
    dma = pltpu.SemaphoreType.DMA
    return pl.pallas_call(
        kernel,
        out_shape=jax.ShapeDtypeStruct(vectors.shape, F32),
        in_specs=[in_hbm] * 12,
        out_specs=pl.BlockSpec(memory_space=pltpu.VMEM),
        scratch_shapes=[
            pltpu.SMEM(near_list.shape, jnp.int32),
            pltpu.SMEM(leaf_list.shape, jnp.int32),
            pltpu.SMEM(leaf_count.shape, jnp.int32),
            pltpu.SMEM(coarse_list.shape, jnp.int32),
            pltpu.SMEM(coarse_count.shape, jnp.int32),
            pltpu.VMEM((48, ROWS, PTS), F32),
            pltpu.VMEM((24, ROWS, 128), F32),
            pltpu.VMEM(bases.shape, F32),
            pltpu.VMEM(transfers_leaf.shape, F32),
            pltpu.VMEM(transfers_group.shape, F32),
            pltpu.VMEM(near_blocks.shape, F32),
            pltpu.VMEM(leaf_coupling.shape, F32),
            pltpu.VMEM(coarse_coupling.shape, F32),
            pltpu.VMEM((RANK, 4 * PTS), F32),
            pltpu.VMEM((ROWS, 4 * PTS), F32),
            pltpu.VMEM((SUBS, 8, 128), F32),
            pltpu.VMEM((SUBS, 2, 8, 128), F32),
            pltpu.VMEM((8, 128), F32),
            pltpu.VMEM((NZ, NY, 8, 128), F32),
            pltpu.VMEM((SUBS, 8, 128), F32),
            pltpu.SemaphoreType.REGULAR((NZ // 2,)),
            dma((15,)),
            dma((2, 3, SUBS)),
            dma((2, 3, SUBS)),
            dma((SUBS, 2)),
            dma((SUBS, 2)),
            dma((NZ // 2,)),
            dma((NZ // 2,)),
            dma((NZ // 2,)),
            dma((NZ // 2,)),
            dma((SUBS,)),
            dma((SUBS,)),
        ],
        compiler_params=pltpu.CompilerParams(
            collective_id=0, has_side_effects=True, vmem_limit_bytes=60 * 1024 * 1024
        ),
    )(
        near_list,
        leaf_list,
        leaf_count,
        coarse_list,
        coarse_count,
        vectors,
        bases,
        transfers_leaf,
        transfers_group,
        near_blocks,
        leaf_coupling,
        coarse_coupling,
    )


def solution(mesh):
    return jax.shard_map(
        per_device,
        mesh=mesh,
        in_specs=(
            P(None, ("leaf", "sub")),
            P(("leaf", "sub"), None, None),
            P(("leaf", "sub"), None, None),
            P(("leaf", "sub"), None, None),
            P(("leaf", "sub"), None, None),
            P(("leaf", "sub"), None),
            P(("leaf", "sub"), None, None),
            P(("leaf", "sub"), None),
            P(("leaf", "sub")),
            P("leaf", None, None),
            P("leaf", None),
            P("leaf"),
        ),
        out_specs=P(None, ("leaf", "sub")),
        check_vma=False,
    )
```

```python
import functools

import jax
import jax.numpy as jnp
from jax import lax
from jax.experimental import pallas as pl
from jax.experimental.pallas import tpu as pltpu
from jax.sharding import PartitionSpec as P

F32 = jnp.float32
BF16 = jnp.bfloat16
MESH = pl.DeviceIdType.MESH
ROWS = 32
PTS = 256
RANK = 64
SUBS = 4
CORES = 2
NY = 8
NZ = 12
KA = 6
NEAR = 3
K2 = 16
X_ORDER = (1, 3, 2)
DYS = (4, 3, 5, 2, 6, 1, 7)


def split(a):
    high = a.astype(BF16)
    return high, (a - high.astype(F32)).astype(BF16)


def dot(a, b, dim):
    return lax.dot_general(a, b, (((1,), (dim,)), ((), ())), preferred_element_type=F32)


def mul(a, b, dim):
    a_high, a_low = split(a)
    b_high, b_low = split(b)
    return dot(a_high, b_high, dim) + (dot(a_high, b_low, dim) + dot(a_low, b_high, dim))


def kernel(
    near_list_hbm,
    leaf_list_hbm,
    leaf_count_hbm,
    coarse_list_hbm,
    coarse_count_hbm,
    x_hbm,
    bases_hbm,
    tl_hbm,
    tg_hbm,
    near_hbm,
    la_hbm,
    ca_hbm,
    out_ref,
    near_list,
    leaf_list,
    leaf_count,
    coarse_list,
    coarse_count,
    xtab,
    ctab,
    bases,
    tl,
    tg,
    near,
    la,
    ca,
    mfold,
    pre,
    stage,
    rs_in,
    mine,
    table,
    cf_all,
    seen,
    load_sem,
    x_send,
    x_recv,
    rs_send,
    rs_recv,
    z_send,
    z_recv,
    s_send,
    s_recv,
    cf_send,
    cf_recv,
):
    leaf = lax.axis_index("leaf")
    s = lax.axis_index("sub")
    c = lax.rem(leaf, 2)
    y = lax.rem(lax.div(leaf, 2), NY)
    z = lax.div(leaf, 2 * NY)

    def leaf_of(zz, yy, cc):
        return zz * (2 * NY) + yy * 2 + cc

    def sub_at(d):
        return lax.rem(s + d, SUBS)

    sibling = leaf_of(z, y, 1 - c)
    partner = lax.rem(leaf + 192 + 2 * c - 1, 192)
    row = [(d, cc) for d in range(SUBS) for cc in range(CORES) if d + cc]

    def row_dev(d, cc):
        return (sibling if cc else leaf, sub_at(d))

    def plane_dev(p, dy):
        return (leaf_of(p, lax.rem(y + dy, NY), c), s)

    first = lax.rem(z + c, 2)
    below = lax.div(z + c, 2)

    loads = {}

    def load(name, src, dst):
        loads[name] = pltpu.make_async_copy(src, dst, load_sem.at[len(loads)])
        loads[name].start()

    own = (SUBS + s) * 4
    for j in range(4):
        load("x%d" % j, x_hbm.at[:, pl.ds(j * PTS, PTS)], xtab.at[own + j])
    load("bases", bases_hbm, bases)
    load("tl", tl_hbm, tl)
    load("tg", tg_hbm, tg)

    barrier = pltpu.get_barrier_semaphore()

    def greet(dev):
        pl.semaphore_signal(barrier, inc=1, device_id=dev, device_id_type=MESH)

    for d, cc in row:
        greet(row_dev(d, cc))
    greet((partner, s))

    @pl.when(c == 0)
    def _():
        for dy in range(1, NY):
            greet(plane_dev(z, dy))

    def greet_plane(q, carry):
        for dy in range(NY):
            greet(plane_dev(first + 2 * q, dy))
        return carry

    lax.fori_loop(below + 1 - c, NZ // 2, greet_plane, 0)

    for j in range(4):
        loads["x%d" % j].wait()
    loads["bases"].wait()
    pairs = []
    for h in range(2):
        a0 = mul(xtab[own + 2 * h], bases[2 * h], 1)
        a1 = mul(xtab[own + 2 * h + 1], bases[2 * h + 1], 1)
        pairs.append(jnp.concatenate([a0, a1], axis=1))
    c_own = (SUBS + s) * 2
    for h in range(2):
        ctab[c_own + h] = pairs[h]
    loads["tl"].wait()
    loads["tg"].wait()
    fold = mul(tg[0], tl[0], 0)
    partial = mul(jnp.concatenate(pairs, axis=1), fold, 1)
    zero = jnp.zeros_like(partial)
    here = jnp.where(
        c == 0,
        jnp.concatenate([partial, zero], axis=1),
        jnp.concatenate([zero, partial], axis=1),
    )
    stage[...] = here.reshape(SUBS, 8, 128)

    pl.semaphore_wait(barrier, len(row) + 1 + (1 - c) * (NY - 1) + below * NY)

    def remote(src, dst, send, recv, dev):
        return pltpu.make_async_remote_copy(
            src_ref=src,
            dst_ref=dst,
            send_sem=send,
            recv_sem=recv,
            device_id=dev,
            device_id_type=MESH,
        )

    sent = []

    def push(*args):
        cp = remote(*args)
        cp.start()
        sent.append(cp)
        return cp

    rs = [
        push(
            stage.at[sub_at(d)],
            rs_in.at[d, cc],
            rs_send.at[d, cc],
            rs_recv.at[d, cc],
            row_dev(d, cc),
        )
        for d, cc in row
    ]

    def x_part(group, sub):
        return xtab.at[pl.ds((group * SUBS + sub) * 4, 4)]

    def c_part(group, sub):
        return ctab.at[pl.ds((group * SUBS + sub) * 2, 2)]

    def to_sibling(d, sub):
        for i, part in enumerate((x_part, c_part)):
            push(part(1, sub), part(2 * c, sub), x_send.at[i, 1, d], x_recv.at[i, 1, d], (sibling, s))

    def to_row(way, group):
        for i, part in enumerate((x_part, c_part)):
            for d in X_ORDER:
                push(part(group, s), part(group, s), x_send.at[i, way, d], x_recv.at[i, way, d], (leaf, sub_at(d)))

    for i, part in enumerate((x_part, c_part)):
        push(part(1, s), part(2 - 2 * c, s), x_send.at[i, 2, 0], x_recv.at[i, 2, 0], (partner, s))
    to_row(0, 1)
    to_sibling(0, s)

    def tell_plane(q, carry):
        for dy in range(NY):
            pl.semaphore_signal(
                seen.at[lax.div(z, 2)],
                inc=1,
                device_id=plane_dev(first + 2 * q, dy),
                device_id_type=MESH,
            )
        return carry

    lax.fori_loop(0, below, tell_plane, 0)

    load("ca", ca_hbm, ca)
    load("la", la_hbm, la)
    load("near", near_hbm, near)
    lists = (
        (near_list_hbm, near_list),
        (leaf_list_hbm, leaf_list),
        (leaf_count_hbm, leaf_count),
        (coarse_list_hbm, coarse_list),
        (coarse_count_hbm, coarse_count),
    )
    for i, (src, dst) in enumerate(lists):
        load("list%d" % i, src, dst)

    for cp in rs:
        cp.wait_recv()
    tile = stage[s]
    for d, cc in row:
        tile = tile + rs_in[d, cc]
    mine[...] = tile

    @pl.when(c == 0)
    def _():
        table[z, y] = tile

    def tile_to(p, dys):
        half = lax.div(p, 2)
        for dy in dys:
            remote(mine, table.at[z, y], z_send.at[half], z_recv.at[lax.div(z, 2)], plane_dev(p, dy)).start()

    def tile_below(q, carry):
        tile_to(first + 2 * q, DYS + (0,))
        return carry

    lax.fori_loop(0, below, tile_below, 0)

    @pl.when(c == 0)
    def _():
        tile_to(z, DYS)

    for j in range(4):
        mfold[:, j * PTS : (j + 1) * PTS] = mul(fold[:, j * RANK : (j + 1) * RANK], bases[j], 0)

    def arrived(i, way, d, ref):
        remote(ref, ref, x_send.at[i, way, d], x_recv.at[i, way, d], (sibling, s)).wait_recv()

    for d in X_ORDER:
        sub = lax.rem(s + SUBS - d, SUBS)
        arrived(0, 0, d, x_part(1, sub))
        arrived(1, 0, d, c_part(1, sub))
        to_sibling(d, sub)
    arrived(0, 2, 0, x_part(2 * c, s))
    arrived(1, 2, 0, c_part(2 * c, s))
    to_row(2, 2 * c)

    def tiles_at(p, count):
        ref = table.at[0, pl.ds(0, count)]
        half = lax.div(p, 2)
        return remote(ref, ref, z_send.at[half], z_recv.at[half], (sibling, s))

    def own_plane(wait):
        @pl.when(c == 0)
        def _():
            wait(tiles_at(z, NY - 1))

    for i in range(NZ // 2):
        p = z + 2 * i + c

        @pl.when((p > z) & (p < NZ))
        def _():
            pl.semaphore_wait(seen.at[lax.div(p, 2)], NY)
            tile_to(p, DYS + (0,))

    for i in range(NZ // 2):
        p = lax.rem(z + 2 * i + c, NZ)
        if i:
            tiles_at(p, NY).wait_recv()
        else:
            own_plane(lambda cp: cp.wait_recv())

            @pl.when(c == 1)
            def _():
                tiles_at(p, NY).wait_recv()

        part = table.at[p]
        push(part, part, s_send.at[i], s_recv.at[i], (sibling, s))

    for i in range(len(lists)):
        loads["list%d" % i].wait()
    loads["ca"].wait()
    for i in range(NZ // 2):
        part = table.at[lax.rem(z + 2 * i + 1 - c, NZ)]
        remote(part, part, s_send.at[i], s_recv.at[i], (sibling, s)).wait_recv()
    lane8 = lax.broadcasted_iota(jnp.int32, (8, 128), 1)
    pieces = []
    for k in range(0, K2, 2):
        two = []
        for q in (k, k + 1):
            entry = coarse_list[0, q]
            chip = lax.div(entry, 2)
            both = table[lax.div(chip, NY), lax.rem(chip, NY)]
            turned = pltpu.roll(both, 64, 1)
            use = jnp.where(q < coarse_count[0], 1.0, 0.0)
            keep = jnp.where(lax.rem(entry, 2) == q % 2, 1.0, 0.0) * use
            two.append(both * keep + turned * (use - keep))
        pieces.append(jnp.where(lane8 < RANK, two[0], two[1]))
    field = mul(jnp.concatenate(pieces, axis=1), ca[0], 1)
    cf_all[s] = jnp.concatenate([field, jnp.zeros_like(field)], axis=1)
    for d in range(1, SUBS):
        push(cf_all.at[s], cf_all.at[s], cf_send.at[d], cf_recv.at[d], (leaf, sub_at(d)))

    for d in range(SUBS):
        sub = lax.rem(s + SUBS - d, SUBS)
        for i, part in enumerate((x_part, c_part)):
            arrived(i, 1, d, part(2 - 2 * c, sub))
            if d:
                arrived(i, 2, d, part(2 * c, sub))
    lane = lax.broadcasted_iota(jnp.int32, (ROWS, 128), 1)

    def picked(entry, k, use):
        both = ctab[lax.div(entry, 2)]
        turned = pltpu.roll(both, 64, 1)
        keep = jnp.where(lax.rem(entry, 2) == k % 2, 1.0, 0.0) * use
        return both * keep + turned * (use - keep)

    loads["la"].wait()
    loads["near"].wait()
    for j in range(4):
        pieces = []
        for k in range(0, KA, 2):
            lo, hi = (
                picked(leaf_list[j, q], q, jnp.where(q < leaf_count[j], 1.0, 0.0))
                for q in (k, k + 1)
            )
            pieces.append(jnp.where(lane < RANK, lo, hi))
        coupled = mul(jnp.concatenate(pieces, axis=1), la[j], 1)
        far = mul(coupled, bases[j], 0)
        sources = jnp.concatenate([xtab[near_list[j, k]] for k in range(NEAR)], axis=1)
        pre[:, j * PTS : (j + 1) * PTS] = far + mul(sources, near[j], 1)

    for d in range(1, SUBS):
        slot = cf_all.at[lax.rem(s + SUBS - d, SUBS)]
        remote(slot, slot, cf_send.at[d], cf_recv.at[d], (sibling, s)).wait_recv()
    field_all = cf_all[...].reshape(ROWS, 128)[:, :RANK]
    out_ref[...] = pre[...] + mul(field_all, mfold[...], 0)

    for cp in sent:
        cp.wait_send()
    for i in range(NZ // 2):
        if i:
            tiles_at(lax.rem(z + 2 * i + c, NZ), NY).wait_send()
        else:
            own_plane(lambda cp: cp.wait_send())

            @pl.when(c == 1)
            def _():
                tiles_at(lax.rem(z + 1, NZ), NY).wait_send()


def per_device(
    vectors,
    bases,
    transfers_leaf,
    transfers_group,
    near_blocks,
    near_list,
    leaf_coupling,
    leaf_list,
    leaf_count,
    coarse_coupling,
    coarse_list,
    coarse_count,
):
    stay = functools.partial(pltpu.with_memory_space_constraint, memory_space=pltpu.HBM)
    in_hbm = pl.BlockSpec(memory_space=pltpu.HBM)
    dma = pltpu.SemaphoreType.DMA
    return pl.pallas_call(
        kernel,
        out_shape=jax.ShapeDtypeStruct(vectors.shape, F32),
        in_specs=[in_hbm] * 12,
        out_specs=pl.BlockSpec(memory_space=pltpu.VMEM),
        scratch_shapes=[
            pltpu.SMEM(near_list.shape, jnp.int32),
            pltpu.SMEM(leaf_list.shape, jnp.int32),
            pltpu.SMEM(leaf_count.shape, jnp.int32),
            pltpu.SMEM(coarse_list.shape, jnp.int32),
            pltpu.SMEM(coarse_count.shape, jnp.int32),
            pltpu.VMEM((48, ROWS, PTS), F32),
            pltpu.VMEM((24, ROWS, 128), F32),
            pltpu.VMEM(bases.shape, F32),
            pltpu.VMEM(transfers_leaf.shape, F32),
            pltpu.VMEM(transfers_group.shape, F32),
            pltpu.VMEM(near_blocks.shape, F32),
            pltpu.VMEM(leaf_coupling.shape, F32),
            pltpu.VMEM(coarse_coupling.shape, F32),
            pltpu.VMEM((RANK, 4 * PTS), F32),
            pltpu.VMEM((ROWS, 4 * PTS), F32),
            pltpu.VMEM((SUBS, 8, 128), F32),
            pltpu.VMEM((SUBS, 2, 8, 128), F32),
            pltpu.VMEM((8, 128), F32),
            pltpu.VMEM((NZ, NY, 8, 128), F32),
            pltpu.VMEM((SUBS, 8, 128), F32),
            pltpu.SemaphoreType.REGULAR((NZ // 2,)),
            dma((15,)),
            dma((2, 3, SUBS)),
            dma((2, 3, SUBS)),
            dma((SUBS, 2)),
            dma((SUBS, 2)),
            dma((NZ // 2,)),
            dma((NZ // 2,)),
            dma((NZ // 2,)),
            dma((NZ // 2,)),
            dma((SUBS,)),
            dma((SUBS,)),
        ],
        compiler_params=pltpu.CompilerParams(
            collective_id=0, has_side_effects=True, vmem_limit_bytes=32 * 1024 * 1024
        ),
    )(
        stay(near_list),
        stay(leaf_list),
        stay(leaf_count),
        stay(coarse_list),
        coarse_count,
        stay(vectors),
        stay(bases),
        stay(transfers_leaf),
        stay(transfers_group),
        stay(near_blocks),
        stay(leaf_coupling),
        stay(coarse_coupling),
    )


def solution(mesh):
    return jax.shard_map(
        per_device,
        mesh=mesh,
        in_specs=(
            P(None, ("leaf", "sub")),
            P(("leaf", "sub"), None, None),
            P(("leaf", "sub"), None, None),
            P(("leaf", "sub"), None, None),
            P(("leaf", "sub"), None, None),
            P(("leaf", "sub"), None),
            P(("leaf", "sub"), None, None),
            P(("leaf", "sub"), None),
            P(("leaf", "sub")),
            P("leaf", None, None),
            P("leaf", None),
            P("leaf"),
        ),
        out_specs=P(None, ("leaf", "sub")),
        check_vma=False,
    )
```

```python
import functools

import jax
import jax.numpy as jnp
from jax import lax
from jax.experimental import pallas as pl
from jax.experimental.pallas import tpu as pltpu
from jax.sharding import PartitionSpec as P

F32 = jnp.float32
BF16 = jnp.bfloat16
MESH = pl.DeviceIdType.MESH
ROWS = 32
PTS = 256
RANK = 64
SUBS = 4
CORES = 2
NY = 8
NZ = 12
KA = 6
NEAR = 3
K2 = 16
X_ORDER = (1, 3, 2)
YS = (0, 1, 7, 2, 6, 3, 5, 4)
LATE = 10


def split(a):
    high = a.astype(BF16)
    return high, (a - high.astype(F32)).astype(BF16)


def dot(a, b, dim):
    return lax.dot_general(a, b, (((1,), (dim,)), ((), ())), preferred_element_type=F32)


def mul(a, b, dim):
    a_high, a_low = split(a)
    b_high, b_low = split(b)
    return dot(a_high, b_high, dim) + (dot(a_high, b_low, dim) + dot(a_low, b_high, dim))


def mul_parts(a, b_high, b_low, dim):
    rows = a.shape[0]
    a_high, a_low = split(a)
    both = dot(jnp.concatenate([a_high, a_low], axis=0), b_high, dim)
    return both[:rows] + (dot(a_high, b_low, dim) + both[rows:])


def kernel(
    near_list_hbm,
    leaf_list_hbm,
    leaf_count_hbm,
    coarse_list_hbm,
    coarse_count_hbm,
    x_hbm,
    bases_hbm,
    tl_hbm,
    tg_hbm,
    near_hbm,
    la_hbm,
    ca_hbm,
    pre,
    m_ref,
    field_ref,
    near_list,
    leaf_list,
    leaf_count,
    coarse_list,
    coarse_count,
    xtab,
    ctab,
    bases,
    tl,
    tg,
    near,
    la,
    ca,
    near_high,
    near_low,
    ca_high,
    ca_low,
    stage,
    rs_in,
    mine,
    table,
    cf_out,
    cf_in,
    sib_ca,
    sib_list,
    sib_count,
    seen,
    load_sem,
    x_send,
    x_recv,
    rs_send,
    rs_recv,
    z_send,
    z_recv,
    s_send,
    s_recv,
    cf_send,
    cf_recv,
):
    leaf = lax.axis_index("leaf")
    s = lax.axis_index("sub")
    c = lax.rem(leaf, 2)
    y = lax.rem(lax.div(leaf, 2), NY)
    z = lax.div(leaf, 2 * NY)

    def leaf_of(zz, yy, cc):
        return zz * (2 * NY) + yy * 2 + cc

    def sub_at(d):
        return lax.rem(s + d, SUBS)

    sibling = leaf_of(z, y, 1 - c)
    partner = lax.rem(leaf + 192 + 2 * c - 1, 192)
    row = [(d, cc) for d in range(SUBS) for cc in range(CORES) if d + cc]

    def row_dev(d, cc):
        return (sibling if cc else leaf, sub_at(d))

    def plane_dev(p, dy):
        return (leaf_of(p, lax.rem(y + dy, NY), c), s)

    first = lax.rem(z + c, 2)
    below = lax.div(z + c, 2)

    loads = {}

    def load(name, src, dst):
        loads[name] = pltpu.make_async_copy(src, dst, load_sem.at[len(loads)])
        loads[name].start()

    own = (SUBS + s) * 4
    for j in range(4):
        load("x%d" % j, x_hbm.at[:, pl.ds(j * PTS, PTS)], xtab.at[own + j])
    load("bases", bases_hbm, bases)
    load("tl", tl_hbm, tl)
    load("tg", tg_hbm, tg)

    barrier = pltpu.get_barrier_semaphore()

    def greet(dev):
        pl.semaphore_signal(barrier, inc=1, device_id=dev, device_id_type=MESH)

    for d, cc in row:
        greet(row_dev(d, cc))
    greet((partner, s))

    @pl.when(c == 0)
    def _():
        for dy in range(1, NY):
            greet(plane_dev(z, dy))

    def greet_plane(q, carry):
        for dy in range(NY):
            greet(plane_dev(first + 2 * q, dy))
        return carry

    lax.fori_loop(below + 1 - c, NZ // 2, greet_plane, 0)

    for j in range(4):
        loads["x%d" % j].wait()
    loads["bases"].wait()
    pairs = []
    for h in range(2):
        a0 = mul(xtab[own + 2 * h], bases[2 * h], 1)
        a1 = mul(xtab[own + 2 * h + 1], bases[2 * h + 1], 1)
        pairs.append(jnp.concatenate([a0, a1], axis=1))
    c_own = (SUBS + s) * 2
    for h in range(2):
        ctab[c_own + h] = pairs[h]
    loads["tl"].wait()
    loads["tg"].wait()
    fold = mul(tg[0], tl[0], 0)
    partial = mul(jnp.concatenate(pairs, axis=1), fold, 1)
    zero = jnp.zeros_like(partial)
    here = jnp.where(
        c == 0,
        jnp.concatenate([partial, zero], axis=1),
        jnp.concatenate([zero, partial], axis=1),
    )
    stage[...] = here.reshape(SUBS, 8, 128)

    pl.semaphore_wait(barrier, len(row) + 1 + (1 - c) * (NY - 1) + below * NY)

    def remote(src, dst, send, recv, dev):
        return pltpu.make_async_remote_copy(
            src_ref=src,
            dst_ref=dst,
            send_sem=send,
            recv_sem=recv,
            device_id=dev,
            device_id_type=MESH,
        )

    sent = []

    def push(*args):
        cp = remote(*args)
        cp.start()
        sent.append(cp)
        return cp

    rs = [
        push(
            stage.at[sub_at(d)],
            rs_in.at[d, cc],
            rs_send.at[d, cc],
            rs_recv.at[d, cc],
            row_dev(d, cc),
        )
        for d, cc in row
    ]

    def x_part(group, sub):
        return xtab.at[pl.ds((group * SUBS + sub) * 4, 4)]

    def c_part(group, sub):
        return ctab.at[pl.ds((group * SUBS + sub) * 2, 2)]

    def to_sibling(d, sub):
        return [
            remote(part(1, sub), part(2 * c, sub), x_send.at[i, 1, d], x_recv.at[i, 1, d], (sibling, s))
            for i, part in enumerate((x_part, c_part))
        ]

    def to_row(way, group):
        return [
            remote(part(group, s), part(group, s), x_send.at[i, way, d], x_recv.at[i, way, d], (leaf, sub_at(d)))
            for i, part in enumerate((x_part, c_part))
            for d in X_ORDER
        ]

    def arrived(i, way, d, ref):
        remote(ref, ref, x_send.at[i, way, d], x_recv.at[i, way, d], (sibling, s)).wait_recv()

    def start_all(cps):
        for cp in cps:
            cp.start()

    for i, part in enumerate((x_part, c_part)):
        push(part(1, s), part(2 - 2 * c, s), x_send.at[i, 2, 0], x_recv.at[i, 2, 0], (partner, s))
    own_block = to_row(0, 1) + to_sibling(0, s)
    row_blocks = [(d, to_sibling(d, lax.rem(s + SUBS - d, SUBS))) for d in X_ORDER]
    partner_block = to_row(2, 2 * c)
    for cps in [own_block, partner_block] + [cps for _, cps in row_blocks]:
        sent.extend(cps)

    def hand_on():
        arrived(0, 2, 0, x_part(2 * c, s))
        arrived(1, 2, 0, c_part(2 * c, s))
        start_all(partner_block)
        for d, cps in row_blocks:
            sub = lax.rem(s + SUBS - d, SUBS)
            arrived(0, 0, d, x_part(1, sub))
            arrived(1, 0, d, c_part(1, sub))
            start_all(cps)

    late = z >= LATE

    @pl.when(jnp.logical_not(late))
    def _():
        start_all(own_block)

    def tell_plane(q, carry):
        for dy in range(NY):
            pl.semaphore_signal(
                seen.at[lax.div(z, 2)],
                inc=1,
                device_id=plane_dev(first + 2 * q, dy),
                device_id_type=MESH,
            )
        return carry

    lax.fori_loop(0, below, tell_plane, 0)

    load("ca", ca_hbm, ca)
    load("la", la_hbm, la)
    load("near", near_hbm, near)
    lists = (
        (near_list_hbm, near_list),
        (leaf_list_hbm, leaf_list),
        (leaf_count_hbm, leaf_count),
        (coarse_list_hbm, coarse_list),
        (coarse_count_hbm, coarse_count),
    )
    for i, (src, dst) in enumerate(lists):
        load("list%d" % i, src, dst)

    for cp in rs:
        cp.wait_recv()
    tile = stage[s]
    for d, cc in row:
        tile = tile + rs_in[d, cc]
    mine[...] = tile

    @pl.when(c == 0)
    def _():
        table[z, y] = tile

    def tile_to(dev, half):
        remote(mine, table.at[z, y], z_send.at[half], z_recv.at[lax.div(z, 2)], dev).start()

    def tile_to_plane(p):
        for yy in YS:
            tile_to((leaf_of(p, yy, c), s), lax.div(p, 2))

    def tile_below(q, carry):
        tile_to_plane(first + 2 * q)
        return carry

    lax.fori_loop(0, below, tile_below, 0)

    @pl.when(c == 0)
    def _():
        for dy in range(1, NY):
            tile_to(plane_dev(z, dy), lax.div(z, 2))

    for j in range(4):
        piece = mul(fold[:, j * RANK : (j + 1) * RANK], bases[j], 0)
        m_ref[:, j * PTS : (j + 1) * PTS] = piece

    @pl.when(jnp.logical_not(late))
    def _():
        hand_on()

    for name in ("near", "la", "ca"):
        loads[name].wait()
    for i in range(len(lists)):
        loads["list%d" % i].wait()
    for j in range(4):
        near_high[j], near_low[j] = split(near[j])
    shared = ((ca, sib_ca), (coarse_list, sib_list), (coarse_count, sib_count))
    for i, (src, dst) in enumerate(shared):
        push(src, dst, s_send.at[i], s_recv.at[i], (sibling, s))

    def near_field():
        for d in range(SUBS):
            sub = lax.rem(s + SUBS - d, SUBS)
            for i, part in enumerate((x_part, c_part)):
                arrived(i, 1, d, part(2 - 2 * c, sub))
                if d:
                    arrived(i, 2, d, part(2 * c, sub))
        lane = lax.broadcasted_iota(jnp.int32, (ROWS, 128), 1)

        def picked(entry, k, use):
            both = ctab[lax.div(entry, 2)]
            turned = pltpu.roll(both, 64, 1)
            keep = jnp.where(lax.rem(entry, 2) == k % 2, 1.0, 0.0) * use
            return both * keep + turned * (use - keep)

        for j in range(4):
            pieces = []
            for k in range(0, KA, 2):
                lo, hi = (
                    picked(leaf_list[j, q], q, jnp.where(q < leaf_count[j], 1.0, 0.0))
                    for q in (k, k + 1)
                )
                pieces.append(jnp.where(lane < RANK, lo, hi))
            coupled = mul(jnp.concatenate(pieces, axis=1), la[j], 1)
            far = mul(coupled, bases[j], 0)
            sources = jnp.concatenate([xtab[near_list[j, k]] for k in range(NEAR)], axis=1)
            pre[:, j * PTS : (j + 1) * PTS] = far + mul_parts(sources, near_high[j], near_low[j], 1)

    def tiles_at(p, count):
        ref = table.at[0, pl.ds(0, count)]
        half = lax.div(p, 2)
        return remote(ref, ref, z_send.at[half], z_recv.at[half], (sibling, s))

    def own_plane(wait):
        @pl.when(c == 0)
        def _():
            wait(tiles_at(z, NY - 1))

    for i in range(NZ // 2):
        p = z + 2 * i + c

        @pl.when((p > z) & (p < NZ))
        def _():
            pl.semaphore_wait(seen.at[lax.div(p, 2)], NY)
            tile_to_plane(p)

    @pl.when(late)
    def _():
        start_all(own_block)
        hand_on()

    near_last = late | (leaf == 0)

    @pl.when(jnp.logical_not(near_last))
    def _():
        near_field()

    for i, (_, dst) in enumerate(shared):
        remote(dst, dst, s_send.at[i], s_recv.at[i], (sibling, s)).wait_recv()
    ca_high[...], ca_low[...] = split(jnp.concatenate([ca[0], sib_ca[0]], axis=0))
    picked_tiles = []
    for entries, count in ((coarse_list, coarse_count), (sib_list, sib_count)):
        picks = []
        for q in range(K2):
            entry = entries[0, q]
            chip = lax.div(entry, 2)
            plane = lax.div(chip, NY)
            use = (q < count[0]) & (lax.rem(plane + z, 2) == c)
            picks.append((plane, lax.rem(chip, NY), lax.rem(entry, 2) == q % 2, use))
        picked_tiles.append(picks)

    for i in range(NZ // 2):
        p = lax.rem(z + 2 * i + c, NZ)
        if i:
            tiles_at(p, NY).wait_recv()
        else:
            own_plane(lambda cp: cp.wait_recv())

            @pl.when(c == 1)
            def _():
                tiles_at(p, NY).wait_recv()

    lane8 = lax.broadcasted_iota(jnp.int32, (8, 128), 1)

    rows = []
    for picks in picked_tiles:
        pieces = []
        for k in range(0, K2, 2):
            two = []
            for q in (k, k + 1):
                plane, at, same, use = picks[q]
                both = table[plane, at]
                kept = jnp.where(same, both, pltpu.roll(both, 64, 1))
                two.append(jnp.where(use, kept, jnp.zeros_like(kept)))
            pieces.append(jnp.where(lane8 < RANK, two[0], two[1]))
        rows.append(jnp.concatenate(pieces, axis=1))
    fields = mul_parts(jnp.concatenate(rows, axis=0), ca_high[...], ca_low[...], 1)
    cf_out[...] = jnp.where(lane8 < RANK, 0.0, fields[8:])
    for d in range(SUBS):
        push(cf_out, cf_in.at[1, s], cf_send.at[1, d], cf_recv.at[1, d], (sibling, sub_at(d)))
    cf_in[0, s] = jnp.where(lane8 < RANK, fields[:8], 0.0)
    for d in range(1, SUBS):
        push(cf_in.at[0, s], cf_in.at[0, s], cf_send.at[0, d], cf_recv.at[0, d], (leaf, sub_at(d)))

    @pl.when(near_last)
    def _():
        near_field()

    for cc in range(CORES):
        for d in range(1 - cc, SUBS):
            slot = cf_in.at[cc, lax.rem(s + SUBS - d, SUBS)]
            remote(slot, slot, cf_send.at[cc, d], cf_recv.at[cc, d], (sibling, s)).wait_recv()
    both = (cf_in[0] + cf_in[1]).reshape(ROWS, 128)
    field_ref[...] = (both + pltpu.roll(both, 64, 1))[:, :RANK]

    for cp in sent:
        cp.wait_send()
    for i in range(NZ // 2):
        if i:
            tiles_at(lax.rem(z + 2 * i + c, NZ), NY).wait_send()
        else:
            own_plane(lambda cp: cp.wait_send())

            @pl.when(c == 1)
            def _():
                tiles_at(lax.rem(z + 1, NZ), NY).wait_send()


def per_device(
    vectors,
    bases,
    transfers_leaf,
    transfers_group,
    near_blocks,
    near_list,
    leaf_coupling,
    leaf_list,
    leaf_count,
    coarse_coupling,
    coarse_list,
    coarse_count,
):
    stay = functools.partial(pltpu.with_memory_space_constraint, memory_space=pltpu.HBM)
    in_hbm = pl.BlockSpec(memory_space=pltpu.HBM)
    dma = pltpu.SemaphoreType.DMA
    pre, fold, field = pl.pallas_call(
        kernel,
        out_shape=(
            jax.ShapeDtypeStruct(vectors.shape, F32),
            jax.ShapeDtypeStruct((RANK, 4 * PTS), F32),
            jax.ShapeDtypeStruct((ROWS, RANK), F32),
        ),
        in_specs=[in_hbm] * 12,
        out_specs=(pl.BlockSpec(memory_space=pltpu.VMEM),) * 3,
        scratch_shapes=[
            pltpu.SMEM(near_list.shape, jnp.int32),
            pltpu.SMEM(leaf_list.shape, jnp.int32),
            pltpu.SMEM(leaf_count.shape, jnp.int32),
            pltpu.SMEM(coarse_list.shape, jnp.int32),
            pltpu.SMEM(coarse_count.shape, jnp.int32),
            pltpu.VMEM((48, ROWS, PTS), F32),
            pltpu.VMEM((24, ROWS, 128), F32),
            pltpu.VMEM(bases.shape, F32),
            pltpu.VMEM(transfers_leaf.shape, F32),
            pltpu.VMEM(transfers_group.shape, F32),
            pltpu.VMEM(near_blocks.shape, F32),
            pltpu.VMEM(leaf_coupling.shape, F32),
            pltpu.VMEM(coarse_coupling.shape, F32),
            pltpu.VMEM(near_blocks.shape, BF16),
            pltpu.VMEM(near_blocks.shape, BF16),
            pltpu.VMEM((2 * RANK, K2 * RANK), BF16),
            pltpu.VMEM((2 * RANK, K2 * RANK), BF16),
            pltpu.VMEM((SUBS, 8, 128), F32),
            pltpu.VMEM((SUBS, 2, 8, 128), F32),
            pltpu.VMEM((8, 128), F32),
            pltpu.VMEM((NZ, NY, 8, 128), F32),
            pltpu.VMEM((8, 128), F32),
            pltpu.VMEM((CORES, SUBS, 8, 128), F32),
            pltpu.VMEM(coarse_coupling.shape, F32),
            pltpu.SMEM(coarse_list.shape, jnp.int32),
            pltpu.SMEM(coarse_count.shape, jnp.int32),
            pltpu.SemaphoreType.REGULAR((NZ // 2,)),
            dma((15,)),
            dma((2, 3, SUBS)),
            dma((2, 3, SUBS)),
            dma((SUBS, 2)),
            dma((SUBS, 2)),
            dma((NZ // 2,)),
            dma((NZ // 2,)),
            dma((3,)),
            dma((3,)),
            dma((CORES, SUBS)),
            dma((CORES, SUBS)),
        ],
        compiler_params=pltpu.CompilerParams(
            collective_id=0, has_side_effects=True, vmem_limit_bytes=32 * 1024 * 1024
        ),
    )(
        stay(near_list),
        stay(leaf_list),
        stay(leaf_count),
        stay(coarse_list),
        coarse_count,
        stay(vectors),
        stay(bases),
        stay(transfers_leaf),
        stay(transfers_group),
        stay(near_blocks),
        stay(leaf_coupling),
        stay(coarse_coupling),
    )
    return pre + jnp.dot(field, fold, precision=lax.Precision.HIGHEST)


def solution(mesh):
    return jax.shard_map(
        per_device,
        mesh=mesh,
        in_specs=(
            P(None, ("leaf", "sub")),
            P(("leaf", "sub"), None, None),
            P(("leaf", "sub"), None, None),
            P(("leaf", "sub"), None, None),
            P(("leaf", "sub"), None, None),
            P(("leaf", "sub"), None),
            P(("leaf", "sub"), None, None),
            P(("leaf", "sub"), None),
            P(("leaf", "sub")),
            P("leaf", None, None),
            P("leaf", None),
            P("leaf"),
        ),
        out_specs=P(None, ("leaf", "sub")),
        check_vma=False,
    )
```
